32 devices in a mesh: replica: 4 (over z), shard: 8 (over y, x, core).
Axes of the slice: x: 2, y: 2, z: 4, core: 2. Of those that a mesh axis runs over, the one named last changes fastest.
Arguments:
- grads: bfloat16 [4, 2048, 6144], P('replica', 'shard'), may hold values from -3 to 3
- owner_map: int32 [4, 12], replicated, may hold values from 0 to 23, as said below
- factor_left: float32 [32, 3, 512, 512], P(('replica', 'shard')), may hold values from -1 to 7
- factor_right: float32 [32, 3, 512, 512], P(('replica', 'shard')), may hold values from -1 to 7
- left_inverse_roots: bfloat16 [32, 3, 512, 512], P(('replica', 'shard')), may hold values from -1 to 7
- right_inverse_roots: bfloat16 [32, 3, 512, 512], P(('replica', 'shard')), may hold values from -1 to 7
Outputs:
- new_left: float32 [32, 3, 512, 512], P(('replica', 'shard'))
- new_right: float32 [32, 3, 512, 512], P(('replica', 'shard'))
- update: bfloat16 [2048, 6144], P('shard')
The draws below stay inside these ranges and needn't reach their ends.
Inputs may be any that keep to these rules, and one draw needn't show every extreme that they name: `owner_map`: within one block row and one replica's 3 block columns no two blocks name the same owner; within one replica's 3 block columns no two blocks share an entry; some owner holds 3 blocks in every draw.
All inputs are finite; a program needn't handle non-finite values.
Results may differ from the reference program's by a relative error of at most 0.0058.
Values may be sent and summed in bfloat16 or wider, within the bound.
A program may use at most 128 MiB of HBM per device.

```python
import math
import jax
import jax.numpy as jnp
from jax import lax

BS = 512
BR = 4
CAP = 3
REPLICAS = 4
SHARDS = 8
FACTOR_OWNERS = 32
NBC = 12
COLS = 6144
ROWS = 2048


def assemble(key_diag, offdiag, floor_scale, top_scale, spread):
    diagonal = jnp.exp(jax.random.uniform(key_diag, (FACTOR_OWNERS, CAP, BS, 1), jnp.float32, math.log(floor_scale), math.log(top_scale)))
    identity = jnp.eye(BS, dtype=jnp.float32)
    return diagonal * identity + offdiag * (spread / math.sqrt(BS))


def draw_owner_map(key, part):
    key = jax.random.fold_in(key, 7)
    per_group = NBC // REPLICAS
    stride = (per_group + 2) // 3
    columns_list = []
    for group_index in range(REPLICAS):
        middle = jax.random.permutation(jax.random.fold_in(key, 100 + group_index), SHARDS - 2).astype(jnp.int32) + 1
        first = jnp.zeros((1,), jnp.int32)
        last = jnp.full((1,), SHARDS - 1, jnp.int32)
        owners = jnp.concatenate([first, middle[:2 * stride - 1], last, middle[2 * stride - 1:]])
        row_list = []
        for row_index in range(BR):
            ordering = jax.random.permutation(jax.random.fold_in(key, 1000 + group_index * BR + row_index), per_group)
            position = row_index * stride + ordering
            counted = jnp.zeros((per_group,), jnp.int32)
            for earlier in range(row_index):
                counted = counted + (position < earlier * stride + per_group).astype(jnp.int32)
            row_list.append(owners[position] * CAP + counted)
        columns_list.append(jnp.stack(row_list))
    return jnp.concatenate(columns_list, axis=1).astype(jnp.int32)


def draw_factor_left(key, part):
    key = jax.random.fold_in(key, 3)
    key_diag, key_off = jax.random.split(key)
    full_shape = (FACTOR_OWNERS, CAP, BS, BS)
    offdiag = jnp.clip(jax.random.normal(key_off, full_shape, jnp.float32), -4.0, 4.0)
    return assemble(key_diag, offdiag, 0.5, 3.0, 0.3)


def draw_factor_right(key, part):
    key = jax.random.fold_in(key, 4)
    key_diag, key_off = jax.random.split(key)
    full_shape = (FACTOR_OWNERS, CAP, BS, BS)
    offdiag = jnp.clip(jax.random.normal(key_off, full_shape, jnp.float32), -4.0, 4.0)
    return assemble(key_diag, offdiag, 0.5, 3.0, 0.3)


def draw_left_inverse_roots(key, part):
    key = jax.random.fold_in(key, 5)
    key_diag, key_off = jax.random.split(key)
    full_shape = (FACTOR_OWNERS, CAP, BS, BS)
    offdiag = jnp.clip(jax.random.normal(key_off, full_shape, jnp.float32), -4.0, 4.0)
    return assemble(key_diag, offdiag, 0.5, 2.0, 0.6).astype(jnp.bfloat16)


def draw_right_inverse_roots(key, part):
    key = jax.random.fold_in(key, 6)
    key_diag, key_off = jax.random.split(key)
    full_shape = (FACTOR_OWNERS, CAP, BS, BS)
    offdiag = jnp.clip(jax.random.normal(key_off, full_shape, jnp.float32), -4.0, 4.0)
    return assemble(key_diag, offdiag, 0.5, 2.0, 0.6).astype(jnp.bfloat16)


def block_levels(key, shape, shards, low, largest):
    factor_of = 1.0
    for dim, parts in shards:
        steps = jax.random.uniform(jax.random.fold_in(jax.random.fold_in(key, 6), dim), (parts,), jnp.float32, low / len(shards), largest / len(shards))
        factor_of = factor_of * jnp.repeat(jnp.exp(steps), shape[dim] // parts).reshape((-1,) + (1,) * (len(shape) - 1 - dim))
    return factor_of


def bell_draw(own_key, shape, scale, limit, shards=(), held_as=jnp.bfloat16):
    values = scale * jax.random.normal(own_key, shape, jnp.float32)
    if shards:
        values = values * block_levels(own_key, shape, shards, -0.22, 0.18)
    return jnp.clip(values, -limit, limit).astype(held_as)


def setup_inputs(seed: int = 0) -> dict:
    arg_keys = jax.random.split(jax.random.key(seed), 7)
    return {
        "grads": bell_draw(arg_keys[0], (REPLICAS, ROWS, COLS), 0.5, 3.0, ((0, 4), (1, 8))),
        "owner_map": draw_owner_map(jax.random.fold_in(arg_keys[6], 71), 0),
        "factor_left": draw_factor_left(jax.random.fold_in(arg_keys[6], 71), 0),
        "factor_right": draw_factor_right(jax.random.fold_in(arg_keys[6], 71), 0),
        "left_inverse_roots": draw_left_inverse_roots(jax.random.fold_in(arg_keys[6], 71), 0),
        "right_inverse_roots": draw_right_inverse_roots(jax.random.fold_in(arg_keys[6], 71), 0),
    }


def reference(grads, owner_map, factor_left, factor_right, left_inverse_roots, right_inverse_roots):
    summed = jnp.sum(grads.astype(jnp.float32), axis=0)
    blocks = summed.astype(jnp.bfloat16).reshape(BR, BS, NBC, BS).transpose(0, 2, 1, 3).reshape(BR * NBC, BS, BS)
    per_group = NBC // REPLICAS
    column_ids = jnp.arange(NBC, dtype=jnp.int32)
    owner_dev = (column_ids[None, :] // per_group) * SHARDS + owner_map // CAP
    slot_index = (owner_dev * CAP + owner_map % CAP).reshape(-1).astype(jnp.int32)
    left_flat = factor_left.reshape(FACTOR_OWNERS * CAP, BS, BS)
    flattened_right = factor_right.reshape(FACTOR_OWNERS * CAP, BS, BS)
    rootl_flat = left_inverse_roots.reshape(FACTOR_OWNERS * CAP, BS, BS)
    rootr_flat = right_inverse_roots.reshape(FACTOR_OWNERS * CAP, BS, BS)

    def per_block(operand):
        block_grad, where = operand
        left_gram_matrix = jnp.dot(block_grad, block_grad.T, preferred_element_type=jnp.float32)
        right_gram_matrix = jnp.dot(block_grad.T, block_grad, preferred_element_type=jnp.float32)
        preconditioned_update = jnp.dot(rootl_flat[where], block_grad, preferred_element_type=jnp.float32).astype(jnp.bfloat16)
        product = jnp.dot(preconditioned_update, rootr_flat[where], preferred_element_type=jnp.float32).astype(jnp.bfloat16)
        return left_gram_matrix, right_gram_matrix, product

    left_gram_matrix, right_gram_matrix, product = lax.map(per_block, (blocks, slot_index))
    new_left = (0.9 * left_flat).at[slot_index].add((0.1 / BS) * left_gram_matrix)
    new_right = (0.9 * flattened_right).at[slot_index].add((0.1 / BS) * right_gram_matrix)
    update = product.reshape(BR, NBC, BS, BS).transpose(0, 2, 1, 3).reshape(BR * BS, NBC * BS)
    return (new_left.reshape(FACTOR_OWNERS, CAP, BS, BS), new_right.reshape(FACTOR_OWNERS, CAP, BS, BS), update)
```

```python
import jax
import jax.numpy as jnp
from jax import lax
from jax.sharding import PartitionSpec as P


def body(grads, owner_map, factor_left, factor_right, left_roots, right_roots):
    replicas = lax.axis_size("replica")
    shards = lax.axis_size("shard")
    replica_at = lax.axis_index("replica")
    shard_at = lax.axis_index("shard")
    strip_rows, columns = grads.shape[1:]
    capacity, block_size = factor_left.shape[1:3]
    block_rows, block_cols = owner_map.shape
    per_group = block_cols // replicas
    group_entries = lax.dynamic_slice_in_dim(owner_map, replica_at * per_group, per_group, 1)
    row_entries = lax.dynamic_index_in_dim(
        group_entries, shard_at * strip_rows // block_size, 0, keepdims=False
    )
    parts = grads[0].reshape(strip_rows, replicas, per_group, block_size).transpose(1, 2, 0, 3)
    copies = lax.all_to_all(parts, "replica", split_axis=0, concat_axis=0, tiled=True)
    pieces = jnp.sum(copies, axis=0, dtype=jnp.float32).astype(jnp.bfloat16)
    owners = row_entries // capacity
    to_owner = owners[None, :] == jnp.arange(shards, dtype=jnp.int32)[:, None]
    to_owner = to_owner.astype(jnp.bfloat16)
    outgoing = jnp.einsum("dk,kab->dab", to_owner, pieces)
    incoming = lax.all_to_all(outgoing, "shard", split_axis=0, concat_axis=0, tiled=True)
    row_blocks = incoming.reshape(block_rows, block_size, block_size)
    targets = shard_at * capacity + jnp.arange(capacity, dtype=jnp.int32)
    slot_rows = jnp.any(group_entries[None] == targets[:, None, None], axis=2).astype(jnp.bfloat16)
    g = jnp.einsum("ti,iab->tab", slot_rows, row_blocks)
    f32 = dict(preferred_element_type=jnp.float32)
    left_gram = jnp.einsum("tab,tcb->tac", g, g, **f32)
    right_gram = jnp.einsum("tab,tac->tbc", g, g, **f32)
    new_left = 0.9 * factor_left[0] + 0.1 / block_size * left_gram
    new_right = 0.9 * factor_right[0] + 0.1 / block_size * right_gram
    applied = jnp.einsum("tab,tbc->tac", left_roots[0], g, **f32).astype(jnp.bfloat16)
    product = jnp.einsum("tab,tbc->tac", applied, right_roots[0], **f32).astype(jnp.bfloat16)
    by_rows = jnp.einsum("ti,tab->iab", slot_rows, product)
    by_rows = by_rows.reshape(shards, strip_rows, block_size)
    returned = lax.all_to_all(by_rows, "shard", split_axis=0, concat_axis=0, tiled=True)
    own = jnp.einsum("dk,dab->akb", to_owner, returned).reshape(strip_rows, per_group * block_size)
    update = lax.all_gather(own, "replica", axis=1, tiled=True)
    return new_left[None], new_right[None], update


def solution(mesh):
    owned = P(("replica", "shard"), None, None, None)
    in_specs = (P("replica", "shard", None), P(), owned, owned, owned, owned)
    out_specs = (owned, owned, P("shard", None))
    return jax.shard_map(body, mesh=mesh, in_specs=in_specs, out_specs=out_specs, check_vma=False)
```

```python
import functools

import jax
import jax.numpy as jnp
from jax import lax
from jax.experimental import pallas as pl
from jax.experimental.pallas import tpu as pltpu
from jax.sharding import PartitionSpec as P


def plain_body(grads, owner_map, factor_left, factor_right, left_roots, right_roots):
    replicas = lax.axis_size("replica")
    shards = lax.axis_size("shard")
    replica_at = lax.axis_index("replica")
    shard_at = lax.axis_index("shard")
    strip_rows, columns = grads.shape[1:]
    capacity, block_size = factor_left.shape[1:3]
    block_rows, block_cols = owner_map.shape
    per_group = block_cols // replicas
    group_entries = lax.dynamic_slice_in_dim(owner_map, replica_at * per_group, per_group, 1)
    row_entries = lax.dynamic_index_in_dim(
        group_entries, shard_at * strip_rows // block_size, 0, keepdims=False
    )
    parts = grads[0].reshape(strip_rows, replicas, per_group, block_size).transpose(1, 2, 0, 3)
    copies = lax.all_to_all(parts, "replica", split_axis=0, concat_axis=0, tiled=True)
    pieces = jnp.sum(copies, axis=0, dtype=jnp.float32).astype(jnp.bfloat16)
    owners = row_entries // capacity
    to_owner = owners[None, :] == jnp.arange(shards, dtype=jnp.int32)[:, None]
    to_owner = to_owner.astype(jnp.bfloat16)
    outgoing = jnp.einsum("dk,kab->dab", to_owner, pieces)
    incoming = lax.all_to_all(outgoing, "shard", split_axis=0, concat_axis=0, tiled=True)
    row_blocks = incoming.reshape(block_rows, block_size, block_size)
    targets = shard_at * capacity + jnp.arange(capacity, dtype=jnp.int32)
    slot_rows = jnp.any(group_entries[None] == targets[:, None, None], axis=2).astype(jnp.bfloat16)
    g = jnp.einsum("ti,iab->tab", slot_rows, row_blocks)
    f32 = dict(preferred_element_type=jnp.float32)
    left_gram = jnp.einsum("tab,tcb->tac", g, g, **f32)
    right_gram = jnp.einsum("tab,tac->tbc", g, g, **f32)
    new_left = 0.9 * factor_left[0] + 0.1 / block_size * left_gram
    new_right = 0.9 * factor_right[0] + 0.1 / block_size * right_gram
    applied = jnp.einsum("tab,tbc->tac", left_roots[0], g, **f32).astype(jnp.bfloat16)
    product = jnp.einsum("tab,tbc->tac", applied, right_roots[0], **f32).astype(jnp.bfloat16)
    by_rows = jnp.einsum("ti,tab->iab", slot_rows, product)
    by_rows = by_rows.reshape(shards, strip_rows, block_size)
    returned = lax.all_to_all(by_rows, "shard", split_axis=0, concat_axis=0, tiled=True)
    own = jnp.einsum("dk,dab->akb", to_owner, returned).reshape(strip_rows, per_group * block_size)
    update = lax.all_gather(own, "replica", axis=1, tiled=True)
    return new_left[None], new_right[None], update


WIRE = jnp.bfloat16


def exchange_kernel(
    replicas,
    chunks,
    slot_ref,
    valid_ref,
    grads,
    left_roots,
    right_roots,
    update,
    gathered,
    right_in,
    right_out,
    left_in,
    left_out,
    blocks,
    products,
    sib_in,
    half_in,
    whole_in,
    rows_out,
    right_send,
    right_recv,
    left_send,
    left_recv,
    gather_send,
    gather_recv,
    sib_send,
    sib_recv,
    plane_send,
    plane_recv,
    up_send,
    up_recv,
    down_send,
    down_recv,
    block_sem,
    update_sem,
):
    z = lax.axis_index("replica")
    me = lax.axis_index("shard")
    last = replicas - 1
    rows = grads.shape[1]
    half = rows // 2
    size = left_roots.shape[2]
    block_rows = blocks.shape[1] // size

    def other(index, bit):
        return index + bit - 2 * bit * ((index // bit) % 2)

    sib, near_x, near_y = other(me, 1), other(me, 2), other(me, 4)
    diag = other(near_x, 4)

    def at(piece, start=0, count=rows):
        return pl.ds(pl.multiple_of(piece * rows + start, half), count)

    def cols(block):
        return pl.ds(pl.multiple_of(block * size, size), size)

    def remote(src, dst, send, recv, **where):
        return pltpu.make_async_remote_copy(
            src_ref=src,
            dst_ref=dst,
            send_sem=send,
            recv_sem=recv,
            device_id=where,
            device_id_type=pl.DeviceIdType.MESH,
        )

    barrier = pltpu.get_barrier_semaphore()

    def greet(**where):
        pl.semaphore_signal(
            barrier, inc=1, device_id=where, device_id_type=pl.DeviceIdType.MESH
        )

    for neighbour in (sib, near_x, near_y):
        greet(shard=neighbour)
    pl.when(z > 0)(lambda: greet(replica=z - 1))
    pl.when(z < last)(lambda: greet(replica=z + 1))
    ends = (z == 0) | (z == last)
    pl.when(ends)(lambda: pl.semaphore_wait(barrier, 4))
    pl.when(jnp.logical_not(ends))(lambda: pl.semaphore_wait(barrier, 5))

    def to_right(k, d):
        return remote(
            right_out.at[k, d],
            right_in.at[k, d],
            right_send.at[k, d],
            right_recv.at[k, d],
            replica=z + 1,
        )

    def to_left(k, d):
        return remote(
            left_out.at[k, d],
            left_in.at[k, d],
            left_send.at[k, d],
            left_recv.at[k, d],
            replica=z - 1,
        )

    def own(block):
        return grads[0, :, cols(block)].astype(jnp.float32)

    def sum_step(k, j):
        d = last - j

        @pl.when((z < d) & (z == 0))
        def _():
            right_out[k, d] = grads[0, :, cols(d * chunks + k)]
            to_right(k, d).start()

        @pl.when((z < d) & (z > 0))
        def _():
            to_right(k, d).wait_recv()
            total = own(d * chunks + k) + right_in[k, d].astype(jnp.float32)
            right_out[k, d] = total.astype(WIRE)
            to_right(k, d).start()

        e = j

        @pl.when((z > e) & (z == last))
        def _():
            left_out[k, e] = grads[0, :, cols(e * chunks + k)]
            to_left(k, e).start()

        @pl.when((z > e) & (z < last))
        def _():
            to_left(k, e).wait_recv()
            total = own(e * chunks + k) + left_in[k, e].astype(jnp.float32)
            left_out[k, e] = total.astype(WIRE)
            to_left(k, e).start()

    def sum_end(k):
        mine = at(me)

        def store(total):
            blocks[k, mine] = total.astype(jnp.bfloat16)

        @pl.when(z == 0)
        def _():
            to_left(k, z).wait_recv()
            store(own(z * chunks + k) + left_in[k, z].astype(jnp.float32))

        @pl.when(z == last)
        def _():
            to_right(k, z).wait_recv()
            store(own(z * chunks + k) + right_in[k, z].astype(jnp.float32))

        @pl.when((z > 0) & (z < last))
        def _():
            to_right(k, z).wait_recv()
            to_left(k, z).wait_recv()
            store(
                own(z * chunks + k)
                + right_in[k, z].astype(jnp.float32)
                + left_in[k, z].astype(jnp.float32)
            )

    def share(k, n, window, to):
        return remote(
            blocks.at[k, window],
            blocks.at[k, window],
            gather_send.at[k, n],
            gather_recv.at[k, n],
            shard=to,
        )

    def arrived(k, n, window):
        share(k, n, window, sib).wait_recv()

    def gather_1(k):
        share(k, 1, at(me), near_x).start()
        share(k, 2, at(me), near_y).start()
        share(k, 0, at(me), sib).start()

    def gather_2(k):
        arrived(k, 1, at(near_x))
        share(k, 3, at(near_x, 0, half), near_y).start()
        arrived(k, 2, at(near_y))
        share(k, 4, at(near_y, half, half), near_x).start()
        share(k, 5, at(near_x), sib).start()
        share(k, 6, at(near_y), sib).start()

    def gather_3(k):
        arrived(k, 3, at(diag, 0, half))
        arrived(k, 4, at(diag, half, half))
        share(k, 7, at(diag), sib).start()
        arrived(k, 0, at(sib))
        arrived(k, 5, at(other(sib, 2)))
        arrived(k, 6, at(other(sib, 4)))
        arrived(k, 7, at(other(other(sib, 2), 4)))

    def keep_blocks(k):
        return pltpu.make_async_copy(blocks.at[k], gathered.at[k], block_sem.at[k])

    def compute(k):
        keep_blocks(k).start()

        def one(i, carry):
            slot = slot_ref[k * block_rows + i]
            valid = valid_ref[k * block_rows + i]
            window = pl.ds(pl.multiple_of(i * size, size), size)
            applied = jnp.dot(
                left_roots[0, slot], blocks[k, window], preferred_element_type=jnp.float32
            ).astype(jnp.bfloat16)
            product = jnp.dot(
                applied, right_roots[0, slot], preferred_element_type=jnp.float32
            )
            products[k, window] = (product * valid).astype(jnp.bfloat16)
            return carry

        lax.fori_loop(0, block_rows, one, 0)

    sib_pieces = (sib, other(sib, 2), other(sib, 4), other(other(sib, 2), 4))
    own_pieces = (me, near_x, near_y, diag)

    def to_sib(k, j):
        return remote(
            products.at[k, at(sib_pieces[j])],
            sib_in.at[k, j],
            sib_send.at[k, j],
            sib_recv.at[k, j],
            shard=sib,
        )

    def in_plane(k, n):
        source, target, to = (
            (products.at[k, at(diag, 0, half)], half_in.at[k, 0], near_x),
            (products.at[k, at(diag, half, half)], half_in.at[k, 1], near_y),
            (products.at[k, at(near_x)], whole_in.at[k, 0], near_x),
            (products.at[k, at(near_y)], whole_in.at[k, 1], near_y),
        )[n]
        return remote(source, target, plane_send.at[k, n], plane_recv.at[k, n], shard=to)

    def reduce_1(k):
        for j in (3, 2, 1, 0):
            to_sib(k, j).start()

    def reduce_2(k):
        for j in (3, 2, 1, 0):
            to_sib(k, j).wait_recv()
            window = at(own_pieces[j])
            products[k, window] = products[k, window] + sib_in[k, j]
            if j == 3:
                in_plane(k, 0).start()
                in_plane(k, 1).start()

    def reduce_3(k):
        in_plane(k, 1).wait_recv()
        window = at(near_x, half, half)
        products[k, window] = products[k, window] + half_in[k, 1]
        in_plane(k, 2).start()
        in_plane(k, 0).wait_recv()
        window = at(near_y, 0, half)
        products[k, window] = products[k, window] + half_in[k, 0]
        in_plane(k, 3).start()

    def go_up(k, origin):
        block = origin * chunks + k
        return remote(
            rows_out.at[block],
            rows_out.at[block],
            up_send.at[block],
            up_recv.at[block],
            replica=z + 1,
        )

    def go_down(k, origin):
        block = origin * chunks + k
        return remote(
            rows_out.at[block],
            rows_out.at[block],
            down_send.at[block],
            down_recv.at[block],
            replica=z - 1,
        )

    def write(k, origin):
        block = origin * chunks + k
        return pltpu.make_async_copy(
            rows_out.at[block], update.at[:, cols(block)], update_sem.at[block]
        )

    def reduce_4(k):
        in_plane(k, 2).wait_recv()
        in_plane(k, 3).wait_recv()
        rows_out[z * chunks + k] = products[k, at(me)] + whole_in[k, 0] + whole_in[k, 1]
        pl.when(z < last)(lambda: go_up(k, z).start())
        pl.when(z > 0)(lambda: go_down(k, z).start())
        write(k, z).start()

    def spread(k, hop):
        @pl.when(z >= hop)
        def _():
            go_up(k, z - hop).wait_recv()
            pl.when(z < last)(lambda: go_up(k, z - hop).start())
            write(k, z - hop).start()

        @pl.when(z + hop <= last)
        def _():
            go_down(k, z + hop).wait_recv()
            pl.when(z > 0)(lambda: go_down(k, z + hop).start())
            write(k, z + hop).start()

    steps = [functools.partial(sum_step, j=j) for j in range(last)]

    def finish_sum(k):
        sum_end(k)
        gather_1(k)

    def middle(k):
        gather_3(k)
        compute(k)
        reduce_1(k)

    stages = steps[:-1] + [lambda k: (steps[-1](k), finish_sum(k))]
    stages += [gather_2, middle, reduce_2, reduce_3, reduce_4]
    stages += [functools.partial(spread, hop=hop) for hop in range(1, last + 1)]
    for tick in range(len(stages) + last * (chunks - 1)):
        for k in reversed(range(chunks)):
            stage = tick - last * k
            if 0 <= stage < len(stages):
                stages[stage](k)

    for k in range(chunks):
        for d in range(replicas):
            pl.when(z < d)(lambda: to_right(k, d).wait_send())
            pl.when(z > d)(lambda: to_left(k, d).wait_send())
            pl.when((z < last) & (z >= d))(lambda: go_up(k, d).wait_send())
            pl.when((z > 0) & (z <= d))(lambda: go_down(k, d).wait_send())
            write(k, d).wait()
        share(k, 0, at(me), sib).wait_send()
        share(k, 1, at(me), near_x).wait_send()
        share(k, 2, at(me), near_y).wait_send()
        share(k, 3, at(near_x, 0, half), near_y).wait_send()
        share(k, 4, at(near_y, half, half), near_x).wait_send()
        share(k, 5, at(near_x), sib).wait_send()
        share(k, 6, at(near_y), sib).wait_send()
        share(k, 7, at(diag), sib).wait_send()
        for n in range(4):
            to_sib(k, n).wait_send()
            in_plane(k, n).wait_send()
        keep_blocks(k).wait()


def gram_kernel(size, place, valid, block, left, right, new_left, new_right):
    t = pl.program_id(0)
    g = block[0]
    scale = 0.1 / size * valid[t].astype(jnp.float32)
    f32 = dict(preferred_element_type=jnp.float32)
    left_gram = lax.dot_general(g, g, (((1,), (1,)), ((), ())), **f32)
    new_left[0] = 0.9 * left[0] + scale * left_gram
    right_gram = lax.dot_general(g, g, (((0,), (0,)), ((), ())), **f32)
    new_right[0] = 0.9 * right[0] + scale * right_gram


def line_body(grads, owner_map, factor_left, factor_right, left_roots, right_roots):
    replicas = lax.axis_size("replica")
    shards = lax.axis_size("shard")
    replica_at = lax.axis_index("replica")
    shard_at = lax.axis_index("shard")
    rows, columns = grads.shape[1:]
    capacity, size = factor_left.shape[1:3]
    block_rows, block_cols = owner_map.shape
    chunks = block_cols // replicas
    total_rows = rows * shards
    group = lax.dynamic_slice_in_dim(owner_map, replica_at * chunks, chunks, 1).T.reshape(-1)
    mine = group // capacity == shard_at
    slots = jnp.where(mine, group % capacity, 0)
    vmem = pl.BlockSpec(memory_space=pltpu.VMEM)
    smem = pl.BlockSpec(memory_space=pltpu.SMEM)
    hbm = pl.BlockSpec(memory_space=pl.ANY)
    dma = pltpu.SemaphoreType.DMA
    piece = (rows, size)
    bf16 = jnp.bfloat16
    update, gathered = pl.pallas_call(
        functools.partial(exchange_kernel, replicas, chunks),
        out_shape=(
            jax.ShapeDtypeStruct((rows, columns), bf16),
            jax.ShapeDtypeStruct((chunks, total_rows, size), bf16),
        ),
        in_specs=[smem, smem, vmem, vmem, vmem],
        out_specs=(hbm, hbm),
        scratch_shapes=[pltpu.VMEM((chunks, replicas) + piece, WIRE)] * 4
        + [pltpu.VMEM((chunks, total_rows, size), bf16)] * 2
        + [
            pltpu.VMEM((chunks, 4) + piece, bf16),
            pltpu.VMEM((chunks, 2, rows // 2, size), bf16),
            pltpu.VMEM((chunks, 2) + piece, bf16),
            pltpu.VMEM((block_cols,) + piece, bf16),
        ]
        + [dma((chunks, replicas))] * 4
        + [dma((chunks, 8))] * 2
        + [dma((chunks, 4))] * 4
        + [dma((block_cols,))] * 4
        + [dma((chunks,)), dma((block_cols,))],
        compiler_params=pltpu.CompilerParams(
            collective_id=0, has_side_effects=True, vmem_limit_bytes=56 * 2**20
        ),
        name="exchange",
    )(slots, mine.astype(jnp.float32), grads, left_roots, right_roots)

    targets = shard_at * capacity + jnp.arange(capacity, dtype=jnp.int32)
    hits = group[None, :] == targets[:, None]
    place = jnp.sum(jnp.where(hits, jnp.arange(group.shape[0], dtype=jnp.int32), 0), axis=1)
    valid = jnp.any(hits, axis=1).astype(jnp.int32)
    square = pl.BlockSpec((1, size, size), lambda t, place, valid: (t, 0, 0))
    chosen = pl.BlockSpec(
        (1, size, size),
        lambda t, place, valid: (place[t] // block_rows, place[t] % block_rows, 0),
    )
    factor = jax.ShapeDtypeStruct(factor_left.shape[1:], jnp.float32)
    new_left, new_right = pl.pallas_call(
        functools.partial(gram_kernel, size),
        out_shape=(factor, factor),
        grid_spec=pltpu.PrefetchScalarGridSpec(
            num_scalar_prefetch=2,
            grid=(capacity,),
            in_specs=[chosen, square, square],
            out_specs=(square, square),
        ),
        compiler_params=pltpu.CompilerParams(vmem_limit_bytes=32 * 2**20),
        name="grams",
    )(place, valid, gathered, factor_left[0], factor_right[0])
    return new_left[None], new_right[None], update


def solution(mesh):
    owned = P(("replica", "shard"), None, None, None)
    in_specs = (P("replica", "shard", None), P(), owned, owned, owned, owned)
    out_specs = (owned, owned, P("shard", None))
    body = line_body if mesh.shape["shard"] == 8 else plain_body
    return jax.shard_map(body, mesh=mesh, in_specs=in_specs, out_specs=out_specs, check_vma=False)
```

```python
import functools

import jax
import jax.numpy as jnp
from jax import lax
from jax.experimental import pallas as pl
from jax.experimental.pallas import tpu as pltpu
from jax.sharding import PartitionSpec as P


def plain_body(grads, owner_map, factor_left, factor_right, left_roots, right_roots):
    replicas = lax.axis_size("replica")
    shards = lax.axis_size("shard")
    replica_at = lax.axis_index("replica")
    shard_at = lax.axis_index("shard")
    strip_rows, columns = grads.shape[1:]
    capacity, block_size = factor_left.shape[1:3]
    block_rows, block_cols = owner_map.shape
    per_group = block_cols // replicas
    group_entries = lax.dynamic_slice_in_dim(owner_map, replica_at * per_group, per_group, 1)
    row_entries = lax.dynamic_index_in_dim(
        group_entries, shard_at * strip_rows // block_size, 0, keepdims=False
    )
    parts = grads[0].reshape(strip_rows, replicas, per_group, block_size).transpose(1, 2, 0, 3)
    copies = lax.all_to_all(parts, "replica", split_axis=0, concat_axis=0, tiled=True)
    pieces = jnp.sum(copies, axis=0, dtype=jnp.float32).astype(jnp.bfloat16)
    owners = row_entries // capacity
    to_owner = owners[None, :] == jnp.arange(shards, dtype=jnp.int32)[:, None]
    to_owner = to_owner.astype(jnp.bfloat16)
    outgoing = jnp.einsum("dk,kab->dab", to_owner, pieces)
    incoming = lax.all_to_all(outgoing, "shard", split_axis=0, concat_axis=0, tiled=True)
    row_blocks = incoming.reshape(block_rows, block_size, block_size)
    targets = shard_at * capacity + jnp.arange(capacity, dtype=jnp.int32)
    slot_rows = jnp.any(group_entries[None] == targets[:, None, None], axis=2).astype(jnp.bfloat16)
    g = jnp.einsum("ti,iab->tab", slot_rows, row_blocks)
    f32 = dict(preferred_element_type=jnp.float32)
    left_gram = jnp.einsum("tab,tcb->tac", g, g, **f32)
    right_gram = jnp.einsum("tab,tac->tbc", g, g, **f32)
    new_left = 0.9 * factor_left[0] + 0.1 / block_size * left_gram
    new_right = 0.9 * factor_right[0] + 0.1 / block_size * right_gram
    applied = jnp.einsum("tab,tbc->tac", left_roots[0], g, **f32).astype(jnp.bfloat16)
    product = jnp.einsum("tab,tbc->tac", applied, right_roots[0], **f32).astype(jnp.bfloat16)
    by_rows = jnp.einsum("ti,tab->iab", slot_rows, product)
    by_rows = by_rows.reshape(shards, strip_rows, block_size)
    returned = lax.all_to_all(by_rows, "shard", split_axis=0, concat_axis=0, tiled=True)
    own = jnp.einsum("dk,dab->akb", to_owner, returned).reshape(strip_rows, per_group * block_size)
    update = lax.all_gather(own, "replica", axis=1, tiled=True)
    return new_left[None], new_right[None], update


WIRE = jnp.bfloat16


def exchange_kernel(
    replicas,
    chunks,
    slot_ref,
    valid_ref,
    place_ref,
    held_ref,
    grads,
    left_roots,
    right_roots,
    update,
    picked,
    right_in,
    right_out,
    left_in,
    left_out,
    blocks,
    products,
    sib_in,
    half_in,
    whole_in,
    rows_out,
    right_send,
    right_recv,
    left_send,
    left_recv,
    gather_send,
    gather_recv,
    sib_send,
    sib_recv,
    plane_send,
    plane_recv,
    up_send,
    up_recv,
    down_send,
    down_recv,
    update_sem,
):
    z = lax.axis_index("replica")
    me = lax.axis_index("shard")
    last = replicas - 1
    rows = grads.shape[1]
    half = rows // 2
    size = left_roots.shape[2]
    block_rows = blocks.shape[0] // chunks

    def other(index, bit):
        return index + bit - 2 * bit * ((index // bit) % 2)

    sib, near_x, near_y = other(me, 1), other(me, 2), other(me, 4)
    diag = other(near_x, 4)

    def at(piece, start=0, count=rows):
        return pl.ds(pl.multiple_of(piece * rows + start, half), count)

    def spot(piece, start=0, count=rows):
        per = size // rows
        first = pl.multiple_of((piece % per) * rows + start, half)
        return lambda k: (k * block_rows + piece // per, pl.ds(first, count))

    def cols(block):
        return pl.ds(pl.multiple_of(block * size, size), size)

    def remote(src, dst, send, recv, **where):
        return pltpu.make_async_remote_copy(
            src_ref=src,
            dst_ref=dst,
            send_sem=send,
            recv_sem=recv,
            device_id=where,
            device_id_type=pl.DeviceIdType.MESH,
        )

    barrier = pltpu.get_barrier_semaphore()

    def greet(**where):
        pl.semaphore_signal(
            barrier, inc=1, device_id=where, device_id_type=pl.DeviceIdType.MESH
        )

    for neighbour in (sib, near_x, near_y):
        greet(shard=neighbour)
    pl.when(z > 0)(lambda: greet(replica=z - 1))
    pl.when(z < last)(lambda: greet(replica=z + 1))
    ends = (z == 0) | (z == last)
    pl.when(ends)(lambda: pl.semaphore_wait(barrier, 4))
    pl.when(jnp.logical_not(ends))(lambda: pl.semaphore_wait(barrier, 5))

    def to_right(k, d):
        return remote(
            right_out.at[k, d],
            right_in.at[k, d],
            right_send.at[k, d],
            right_recv.at[k, d],
            replica=z + 1,
        )

    def to_left(k, d):
        return remote(
            left_out.at[k, d],
            left_in.at[k, d],
            left_send.at[k, d],
            left_recv.at[k, d],
            replica=z - 1,
        )

    def own(block):
        return grads[0, :, cols(block)].astype(jnp.float32)

    def raw_right(k, d):
        right_out[k, d] = grads[0, :, cols(d * chunks + k)]
        to_right(k, d).start()

    def raw_left(k, d):
        left_out[k, d] = grads[0, :, cols(d * chunks + k)]
        to_left(k, d).start()

    def pass_right(k, d):
        to_right(k, d).wait_recv()
        total = own(d * chunks + k) + right_in[k, d].astype(jnp.float32)
        right_out[k, d] = total.astype(WIRE)
        to_right(k, d).start()

    def pass_left(k, d):
        to_left(k, d).wait_recv()
        total = own(d * chunks + k) + left_in[k, d].astype(jnp.float32)
        left_out[k, d] = total.astype(WIRE)
        to_left(k, d).start()

    def sum_begin():
        @pl.when(z == 0)
        def _():
            for d in (3, 2, 1):
                raw_right(0, d)

        @pl.when(z == 3)
        def _():
            for d in (0, 1, 2):
                raw_left(0, d)

    def sum_step(k, j):
        @pl.when(z == 0)
        def _():
            to_right(k, 3 - j).wait_send()
            if k + 1 < chunks:
                raw_right(k + 1, 3 - j)

        @pl.when(z == 3)
        def _():
            to_left(k, j).wait_send()
            if k + 1 < chunks:
                raw_left(k + 1, j)

        @pl.when(z == 1)
        def _():
            if j < 2:
                pass_right(k, 3 - j)
            if j == 1:
                pass_left(k, 0)

        @pl.when(z == 2)
        def _():
            if j < 2:
                pass_left(k, j)
            if j == 1:
                pass_right(k, 3)

    def sum_end(k):
        mine = spot(me)(k)

        def store(total):
            blocks[mine] = total.astype(jnp.bfloat16)

        @pl.when(z == 0)
        def _():
            to_left(k, z).wait_recv()
            store(own(z * chunks + k) + left_in[k, z].astype(jnp.float32))

        @pl.when(z == last)
        def _():
            to_right(k, z).wait_recv()
            store(own(z * chunks + k) + right_in[k, z].astype(jnp.float32))

        @pl.when((z > 0) & (z < last))
        def _():
            to_right(k, z).wait_recv()
            to_left(k, z).wait_recv()
            store(
                own(z * chunks + k)
                + right_in[k, z].astype(jnp.float32)
                + left_in[k, z].astype(jnp.float32)
            )

    def share(k, n, window, to):
        there = blocks.at[window(k)]
        return remote(
            there,
            there,
            gather_send.at[k, n],
            gather_recv.at[k, n],
            shard=to,
        )

    def arrived(k, n, window):
        share(k, n, window, sib).wait_recv()

    def gather_1(k):
        share(k, 1, spot(me), near_x).start()
        share(k, 2, spot(me), near_y).start()
        share(k, 0, spot(me), sib).start()

    def gather_2(k):
        arrived(k, 1, spot(near_x))
        share(k, 3, spot(near_x, 0, half), near_y).start()
        arrived(k, 2, spot(near_y))
        share(k, 4, spot(near_y, half, half), near_x).start()
        share(k, 5, spot(near_x), sib).start()
        share(k, 6, spot(near_y), sib).start()

    def gather_3(k):
        arrived(k, 3, spot(diag, 0, half))
        arrived(k, 4, spot(diag, half, half))
        share(k, 7, spot(diag), sib).start()
        arrived(k, 0, spot(sib))
        arrived(k, 5, spot(other(sib, 2)))
        arrived(k, 6, spot(other(sib, 4)))
        arrived(k, 7, spot(other(other(sib, 2), 4)))

    def pick():
        for t in range(picked.shape[0]):
            block = blocks[place_ref[t]]
            picked[t] = (block.astype(jnp.float32) * held_ref[t]).astype(jnp.bfloat16)

    def compute(k):
        def one(i, carry):
            slot = slot_ref[k * block_rows + i]
            valid = valid_ref[k * block_rows + i]
            window = pl.ds(pl.multiple_of(i * size, size), size)
            applied = jnp.dot(
                left_roots[0, slot], blocks[k * block_rows + i], preferred_element_type=jnp.float32
            ).astype(jnp.bfloat16)
            product = jnp.dot(
                applied, right_roots[0, slot], preferred_element_type=jnp.float32
            )
            products[k, window] = (product * valid).astype(jnp.bfloat16)
            return carry

        lax.fori_loop(0, block_rows, one, 0)

    sib_pieces = (sib, other(sib, 2), other(sib, 4), other(other(sib, 2), 4))
    own_pieces = (me, near_x, near_y, diag)

    def to_sib(k, j):
        return remote(
            products.at[k, at(sib_pieces[j])],
            sib_in.at[k, j],
            sib_send.at[k, j],
            sib_recv.at[k, j],
            shard=sib,
        )

    def in_plane(k, n):
        source, target, to = (
            (products.at[k, at(diag, 0, half)], half_in.at[k, 0], near_x),
            (products.at[k, at(diag, half, half)], half_in.at[k, 1], near_y),
            (products.at[k, at(near_x)], whole_in.at[k, 0], near_x),
            (products.at[k, at(near_y)], whole_in.at[k, 1], near_y),
        )[n]
        return remote(source, target, plane_send.at[k, n], plane_recv.at[k, n], shard=to)

    def reduce_1(k):
        for j in (3, 2, 1, 0):
            to_sib(k, j).start()

    def reduce_2(k):
        for j in (3, 2, 1, 0):
            to_sib(k, j).wait_recv()
            window = at(own_pieces[j])
            products[k, window] = products[k, window] + sib_in[k, j]
            if j == 3:
                in_plane(k, 0).start()
                in_plane(k, 1).start()

    def reduce_3(k):
        in_plane(k, 1).wait_recv()
        window = at(near_x, half, half)
        products[k, window] = products[k, window] + half_in[k, 1]
        in_plane(k, 2).start()
        in_plane(k, 0).wait_recv()
        window = at(near_y, 0, half)
        products[k, window] = products[k, window] + half_in[k, 0]
        in_plane(k, 3).start()

    def go_up(k, origin):
        block = origin * chunks + k
        return remote(
            rows_out.at[block],
            rows_out.at[block],
            up_send.at[block],
            up_recv.at[block],
            replica=z + 1,
        )

    def go_down(k, origin):
        block = origin * chunks + k
        return remote(
            rows_out.at[block],
            rows_out.at[block],
            down_send.at[block],
            down_recv.at[block],
            replica=z - 1,
        )

    def write(k, origin):
        block = origin * chunks + k
        return pltpu.make_async_copy(
            rows_out.at[block], update.at[:, cols(block)], update_sem.at[block]
        )

    def reduce_4(k):
        in_plane(k, 2).wait_recv()
        in_plane(k, 3).wait_recv()
        rows_out[z * chunks + k] = products[k, at(me)] + whole_in[k, 0] + whole_in[k, 1]
        pl.when(z < last)(lambda: go_up(k, z).start())
        pl.when(z > 0)(lambda: go_down(k, z).start())
        write(k, z).start()

    def spread(k, hop):
        @pl.when(z >= hop)
        def _():
            go_up(k, z - hop).wait_recv()
            pl.when(z < last)(lambda: go_up(k, z - hop).start())
            write(k, z - hop).start()

        @pl.when(z + hop <= last)
        def _():
            go_down(k, z + hop).wait_recv()
            pl.when(z > 0)(lambda: go_down(k, z + hop).start())
            write(k, z + hop).start()

    steps = [functools.partial(sum_step, j=j) for j in range(last)]

    def finish_sum(k):
        sum_end(k)
        gather_1(k)

    def middle(k):
        gather_3(k)
        compute(k)
        reduce_1(k)

    stages = steps[:-1] + [lambda k: (steps[-1](k), finish_sum(k))]
    stages += [gather_2, middle, reduce_2, reduce_3, reduce_4]
    stages += [functools.partial(spread, hop=hop) for hop in range(1, last + 1)]
    sum_begin()
    for tick in range(len(stages) + last * (chunks - 1)):
        for k in reversed(range(chunks)):
            stage = tick - last * k
            if 0 <= stage < len(stages):
                stages[stage](k)
            if stage == len(stages) - last and k == chunks - 1:
                pick()

    for k in range(chunks):
        for d in range(replicas):
            pl.when((z > 0) & (z < d))(lambda: to_right(k, d).wait_send())
            pl.when((z < last) & (z > d))(lambda: to_left(k, d).wait_send())
            pl.when((z < last) & (z >= d))(lambda: go_up(k, d).wait_send())
            pl.when((z > 0) & (z <= d))(lambda: go_down(k, d).wait_send())
            write(k, d).wait()
        share(k, 0, spot(me), sib).wait_send()
        share(k, 1, spot(me), near_x).wait_send()
        share(k, 2, spot(me), near_y).wait_send()
        share(k, 3, spot(near_x, 0, half), near_y).wait_send()
        share(k, 4, spot(near_y, half, half), near_x).wait_send()
        share(k, 5, spot(near_x), sib).wait_send()
        share(k, 6, spot(near_y), sib).wait_send()
        share(k, 7, spot(diag), sib).wait_send()
        for n in range(4):
            to_sib(k, n).wait_send()
            in_plane(k, n).wait_send()


def gram_kernel(size, block, left, right, new_left, new_right):
    g = block[0]
    scale = 0.1 / size
    f32 = dict(preferred_element_type=jnp.float32)
    left_gram = lax.dot_general(g, g, (((1,), (1,)), ((), ())), **f32)
    new_left[0] = 0.9 * left[0] + scale * left_gram
    right_gram = lax.dot_general(g, g, (((0,), (0,)), ((), ())), **f32)
    new_right[0] = 0.9 * right[0] + scale * right_gram


def line_body(grads, owner_map, factor_left, factor_right, left_roots, right_roots):
    replicas = lax.axis_size("replica")
    shards = lax.axis_size("shard")
    replica_at = lax.axis_index("replica")
    shard_at = lax.axis_index("shard")
    rows, columns = grads.shape[1:]
    capacity, size = factor_left.shape[1:3]
    block_rows, block_cols = owner_map.shape
    chunks = block_cols // replicas
    total_rows = rows * shards
    group = lax.dynamic_slice_in_dim(owner_map, replica_at * chunks, chunks, 1).T.reshape(-1)
    mine = group // capacity == shard_at
    slots = jnp.where(mine, group % capacity, 0)
    targets = shard_at * capacity + jnp.arange(capacity, dtype=jnp.int32)
    hits = group[None, :] == targets[:, None]
    place = jnp.sum(jnp.where(hits, jnp.arange(group.shape[0], dtype=jnp.int32), 0), axis=1)
    held = jnp.any(hits, axis=1).astype(jnp.float32)
    vmem = pl.BlockSpec(memory_space=pltpu.VMEM)
    smem = pl.BlockSpec(memory_space=pltpu.SMEM)
    hbm = pl.BlockSpec(memory_space=pl.ANY)
    dma = pltpu.SemaphoreType.DMA
    piece = (rows, size)
    bf16 = jnp.bfloat16
    update, picked = pl.pallas_call(
        functools.partial(exchange_kernel, replicas, chunks),
        out_shape=(
            jax.ShapeDtypeStruct((rows, columns), bf16),
            jax.ShapeDtypeStruct((capacity, size, size), bf16),
        ),
        in_specs=[smem] * 4 + [vmem] * 3,
        out_specs=(hbm, vmem),
        scratch_shapes=[pltpu.VMEM((chunks, replicas) + piece, WIRE)] * 4
        + [
            pltpu.VMEM((chunks * block_rows, size, size), bf16),
            pltpu.VMEM((chunks, total_rows, size), bf16),
        ]
        + [
            pltpu.VMEM((chunks, 4) + piece, bf16),
            pltpu.VMEM((chunks, 2, rows // 2, size), bf16),
            pltpu.VMEM((chunks, 2) + piece, bf16),
            pltpu.VMEM((block_cols,) + piece, bf16),
        ]
        + [dma((chunks, replicas))] * 4
        + [dma((chunks, 8))] * 2
        + [dma((chunks, 4))] * 4
        + [dma((block_cols,))] * 4
        + [dma((block_cols,))],
        compiler_params=pltpu.CompilerParams(
            collective_id=0, has_side_effects=True, vmem_limit_bytes=56 * 2**20
        ),
        name="exchange",
    )(slots, mine.astype(jnp.float32), place, held, grads, left_roots, right_roots)

    square = pl.BlockSpec((1, size, size), lambda t: (t, 0, 0))
    factor = jax.ShapeDtypeStruct(factor_left.shape[1:], jnp.float32)
    new_left, new_right = pl.pallas_call(
        functools.partial(gram_kernel, size),
        out_shape=(factor, factor),
        grid=(capacity,),
        in_specs=[square] * 3,
        out_specs=(square, square),
        compiler_params=pltpu.CompilerParams(vmem_limit_bytes=32 * 2**20),
        name="grams",
    )(picked, factor_left[0], factor_right[0])
    return new_left[None], new_right[None], update


def solution(mesh):
    owned = P(("replica", "shard"), None, None, None)
    in_specs = (P("replica", "shard", None), P(), owned, owned, owned, owned)
    out_specs = (owned, owned, P("shard", None))
    body = line_body if dict(mesh.shape) == {"replica": 4, "shard": 8} else plain_body
    return jax.shard_map(body, mesh=mesh, in_specs=in_specs, out_specs=out_specs, check_vma=False)
```

```python
import functools

import jax
import jax.numpy as jnp
from jax import lax
from jax.experimental import pallas as pl
from jax.experimental.pallas import tpu as pltpu
from jax.sharding import PartitionSpec as P


def plain_body(grads, owner_map, factor_left, factor_right, left_roots, right_roots):
    replicas = lax.axis_size("replica")
    shards = lax.axis_size("shard")
    replica_at = lax.axis_index("replica")
    shard_at = lax.axis_index("shard")
    strip_rows, columns = grads.shape[1:]
    capacity, block_size = factor_left.shape[1:3]
    block_rows, block_cols = owner_map.shape
    per_group = block_cols // replicas
    group_entries = lax.dynamic_slice_in_dim(owner_map, replica_at * per_group, per_group, 1)
    row_entries = lax.dynamic_index_in_dim(
        group_entries, shard_at * strip_rows // block_size, 0, keepdims=False
    )
    parts = grads[0].reshape(strip_rows, replicas, per_group, block_size).transpose(1, 2, 0, 3)
    copies = lax.all_to_all(parts, "replica", split_axis=0, concat_axis=0, tiled=True)
    pieces = jnp.sum(copies, axis=0, dtype=jnp.float32).astype(jnp.bfloat16)
    owners = row_entries // capacity
    to_owner = owners[None, :] == jnp.arange(shards, dtype=jnp.int32)[:, None]
    to_owner = to_owner.astype(jnp.bfloat16)
    outgoing = jnp.einsum("dk,kab->dab", to_owner, pieces)
    incoming = lax.all_to_all(outgoing, "shard", split_axis=0, concat_axis=0, tiled=True)
    row_blocks = incoming.reshape(block_rows, block_size, block_size)
    targets = shard_at * capacity + jnp.arange(capacity, dtype=jnp.int32)
    slot_rows = jnp.any(group_entries[None] == targets[:, None, None], axis=2).astype(jnp.bfloat16)
    g = jnp.einsum("ti,iab->tab", slot_rows, row_blocks)
    f32 = dict(preferred_element_type=jnp.float32)
    left_gram = jnp.einsum("tab,tcb->tac", g, g, **f32)
    right_gram = jnp.einsum("tab,tac->tbc", g, g, **f32)
    new_left = 0.9 * factor_left[0] + 0.1 / block_size * left_gram
    new_right = 0.9 * factor_right[0] + 0.1 / block_size * right_gram
    applied = jnp.einsum("tab,tbc->tac", left_roots[0], g, **f32).astype(jnp.bfloat16)
    product = jnp.einsum("tab,tbc->tac", applied, right_roots[0], **f32).astype(jnp.bfloat16)
    by_rows = jnp.einsum("ti,tab->iab", slot_rows, product)
    by_rows = by_rows.reshape(shards, strip_rows, block_size)
    returned = lax.all_to_all(by_rows, "shard", split_axis=0, concat_axis=0, tiled=True)
    own = jnp.einsum("dk,dab->akb", to_owner, returned).reshape(strip_rows, per_group * block_size)
    update = lax.all_gather(own, "replica", axis=1, tiled=True)
    return new_left[None], new_right[None], update


WIRE = jnp.bfloat16


def exchange_kernel(
    replicas,
    chunks,
    meta_ref,
    grads,
    left_roots,
    right_roots,
    update,
    picked,
    right_in,
    right_out,
    left_in,
    left_out,
    blocks,
    products,
    sib_in,
    half_in,
    whole_in,
    rows_out,
    right_send,
    right_recv,
    left_send,
    left_recv,
    gather_send,
    gather_recv,
    sib_send,
    sib_recv,
    plane_send,
    plane_recv,
    up_send,
    up_recv,
    down_send,
    down_recv,
    update_sem,
):
    z = lax.axis_index("replica")
    me = lax.axis_index("shard")
    last = replicas - 1
    rows = grads.shape[1]
    half = rows // 2
    size = left_roots.shape[2]
    block_rows = blocks.shape[0] // chunks

    def other(index, bit):
        return index + bit - 2 * bit * ((index // bit) % 2)

    sib, near_x, near_y = other(me, 1), other(me, 2), other(me, 4)
    diag = other(near_x, 4)

    def at(piece, start=0, count=rows):
        return pl.ds(pl.multiple_of(piece * rows + start, half), count)

    def spot(piece, start=0, count=rows):
        per = size // rows
        first = pl.multiple_of((piece % per) * rows + start, half)
        return lambda k: (k * block_rows + piece // per, pl.ds(first, count))

    def cols(block):
        return pl.ds(pl.multiple_of(block * size, size), size)

    def remote(src, dst, send, recv, **where):
        return pltpu.make_async_remote_copy(
            src_ref=src,
            dst_ref=dst,
            send_sem=send,
            recv_sem=recv,
            device_id=where,
            device_id_type=pl.DeviceIdType.MESH,
        )

    barrier = pltpu.get_barrier_semaphore()

    def greet(**where):
        pl.semaphore_signal(
            barrier, inc=1, device_id=where, device_id_type=pl.DeviceIdType.MESH
        )

    for neighbour in (sib, near_x, near_y):
        greet(shard=neighbour)
    pl.when(z > 0)(lambda: greet(replica=z - 1))
    pl.when(z < last)(lambda: greet(replica=z + 1))
    ends = (z == 0) | (z == last)
    pl.when(ends)(lambda: pl.semaphore_wait(barrier, 4))
    pl.when(jnp.logical_not(ends))(lambda: pl.semaphore_wait(barrier, 5))

    def to_right(k, d):
        return remote(
            right_out.at[k, d],
            right_in.at[k, d],
            right_send.at[k, d],
            right_recv.at[k, d],
            replica=z + 1,
        )

    def to_left(k, d):
        return remote(
            left_out.at[k, d],
            left_in.at[k, d],
            left_send.at[k, d],
            left_recv.at[k, d],
            replica=z - 1,
        )

    def own(block):
        return grads[0, :, cols(block)].astype(jnp.float32)

    def raw_right(k, d):
        right_out[k, d] = grads[0, :, cols(d * chunks + k)]
        to_right(k, d).start()

    def raw_left(k, d):
        left_out[k, d] = grads[0, :, cols(d * chunks + k)]
        to_left(k, d).start()

    def pass_right(k, d):
        to_right(k, d).wait_recv()
        total = own(d * chunks + k) + right_in[k, d].astype(jnp.float32)
        right_out[k, d] = total.astype(WIRE)
        to_right(k, d).start()

    def pass_left(k, d):
        to_left(k, d).wait_recv()
        total = own(d * chunks + k) + left_in[k, d].astype(jnp.float32)
        left_out[k, d] = total.astype(WIRE)
        to_left(k, d).start()

    def raw(n):
        k, j = n // 3, n % 3
        pl.when(z == 0)(lambda: raw_right(k, 3 - j))
        pl.when(z == 3)(lambda: raw_left(k, j))

    def sum_step(k, j):
        pl.when(z == 0)(lambda: to_right(k, 3 - j).wait_send())
        pl.when(z == 3)(lambda: to_left(k, j).wait_send())
        n = 3 * k + j
        ready = (n + 1,) if n < 2 else (3, 4) if n == 2 else (n + 2,)
        for later in ready:
            if later < 3 * chunks:
                raw(later)

        @pl.when(z == 1)
        def _():
            if j < 2:
                pass_right(k, 3 - j)
            if j == 1:
                pass_left(k, 0)

        @pl.when(z == 2)
        def _():
            if j < 2:
                pass_left(k, j)
            if j == 1:
                pass_right(k, 3)

    def sum_end(k):
        mine = spot(me)(k)

        def store(total):
            blocks[mine] = total.astype(jnp.bfloat16)

        @pl.when(z == 0)
        def _():
            to_left(k, z).wait_recv()
            store(own(z * chunks + k) + left_in[k, z].astype(jnp.float32))

        @pl.when(z == last)
        def _():
            to_right(k, z).wait_recv()
            store(own(z * chunks + k) + right_in[k, z].astype(jnp.float32))

        @pl.when((z > 0) & (z < last))
        def _():
            to_right(k, z).wait_recv()
            to_left(k, z).wait_recv()
            store(
                own(z * chunks + k)
                + right_in[k, z].astype(jnp.float32)
                + left_in[k, z].astype(jnp.float32)
            )

    def share(k, n, window, to):
        there = blocks.at[window(k)]
        return remote(
            there,
            there,
            gather_send.at[k, n],
            gather_recv.at[k, n],
            shard=to,
        )

    def arrived(k, n, window):
        share(k, n, window, sib).wait_recv()

    def gather_1(k):
        share(k, 1, spot(me), near_x).start()
        share(k, 2, spot(me), near_y).start()
        share(k, 0, spot(me), sib).start()

    def gather_2(k):
        arrived(k, 1, spot(near_x))
        share(k, 3, spot(near_x, 0, half), near_y).start()
        arrived(k, 2, spot(near_y))
        share(k, 4, spot(near_y, half, half), near_x).start()
        share(k, 5, spot(near_x), sib).start()
        share(k, 6, spot(near_y), sib).start()

    def gather_3(k):
        arrived(k, 3, spot(diag, 0, half))
        arrived(k, 4, spot(diag, half, half))
        share(k, 7, spot(diag), sib).start()
        arrived(k, 0, spot(sib))
        arrived(k, 5, spot(other(sib, 2)))
        arrived(k, 6, spot(other(sib, 4)))
        arrived(k, 7, spot(other(other(sib, 2), 4)))

    def pick():
        for t in range(picked.shape[0]):
            place = 2 * chunks * block_rows + t
            held = meta_ref[place + picked.shape[0]].astype(jnp.float32)
            block = blocks[meta_ref[place]]
            picked[t] = (block.astype(jnp.float32) * held).astype(jnp.bfloat16)

    def compute(k):
        def one(i, carry):
            slot = meta_ref[k * block_rows + i]
            valid = meta_ref[(chunks + k) * block_rows + i].astype(jnp.float32)
            window = pl.ds(pl.multiple_of(i * size, size), size)
            applied = jnp.dot(
                left_roots[0, slot], blocks[k * block_rows + i], preferred_element_type=jnp.float32
            ).astype(jnp.bfloat16)
            product = jnp.dot(
                applied, right_roots[0, slot], preferred_element_type=jnp.float32
            )
            products[k, window] = (product * valid).astype(jnp.bfloat16)
            return carry

        lax.fori_loop(0, block_rows, one, 0)

    sib_pieces = (sib, other(sib, 2), other(sib, 4), other(other(sib, 2), 4))
    own_pieces = (me, near_x, near_y, diag)

    def to_sib(k, j):
        return remote(
            products.at[k, at(sib_pieces[j])],
            sib_in.at[k, j],
            sib_send.at[k, j],
            sib_recv.at[k, j],
            shard=sib,
        )

    def in_plane(k, n):
        source, target, to = (
            (products.at[k, at(diag, 0, half)], half_in.at[k, 0], near_x),
            (products.at[k, at(diag, half, half)], half_in.at[k, 1], near_y),
            (products.at[k, at(near_x)], whole_in.at[k, 0], near_x),
            (products.at[k, at(near_y)], whole_in.at[k, 1], near_y),
        )[n]
        return remote(source, target, plane_send.at[k, n], plane_recv.at[k, n], shard=to)

    def reduce_1(k):
        for j in (3, 2, 1, 0):
            to_sib(k, j).start()

    def reduce_2(k):
        for j in (3, 2, 1, 0):
            to_sib(k, j).wait_recv()
            window = at(own_pieces[j])
            products[k, window] = products[k, window] + sib_in[k, j]
            if j == 3:
                in_plane(k, 0).start()
                in_plane(k, 1).start()

    def reduce_3(k):
        in_plane(k, 1).wait_recv()
        window = at(near_x, half, half)
        products[k, window] = products[k, window] + half_in[k, 1]
        in_plane(k, 2).start()
        in_plane(k, 0).wait_recv()
        window = at(near_y, 0, half)
        products[k, window] = products[k, window] + half_in[k, 0]
        in_plane(k, 3).start()

    def go_up(k, origin, p):
        block = origin * chunks + k
        there = rows_out.at[block, pl.ds(p * half, half)]
        return remote(there, there, up_send.at[block, p], up_recv.at[block, p], replica=z + 1)

    def go_down(k, origin, p):
        block = origin * chunks + k
        there = rows_out.at[block, pl.ds(p * half, half)]
        return remote(there, there, down_send.at[block, p], down_recv.at[block, p], replica=z - 1)

    def write(k, origin):
        block = origin * chunks + k
        return pltpu.make_async_copy(
            rows_out.at[block], update.at[:, cols(block)], update_sem.at[block]
        )

    def reduce_4(k):
        in_plane(k, 2).wait_recv()
        in_plane(k, 3).wait_recv()
        rows_out[z * chunks + k] = products[k, at(me)] + whole_in[k, 0] + whole_in[k, 1]
        for p in range(2):
            pl.when(z < last)(lambda: go_up(k, z, p).start())
            pl.when(z > 0)(lambda: go_down(k, z, p).start())
        write(k, z).start()

    def spread(k, hop):
        for p in range(2):

            @pl.when(z >= hop)
            def _():
                go_up(k, z - hop, p).wait_recv()
                pl.when(z < last)(lambda: go_up(k, z - hop, p).start())

            @pl.when(z + hop <= last)
            def _():
                go_down(k, z + hop, p).wait_recv()
                pl.when(z > 0)(lambda: go_down(k, z + hop, p).start())

        pl.when(z >= hop)(lambda: write(k, z - hop).start())
        pl.when(z + hop <= last)(lambda: write(k, z + hop).start())

    steps = [functools.partial(sum_step, j=j) for j in range(last)]

    def finish_sum(k):
        sum_end(k)
        gather_1(k)

    def middle(k):
        gather_3(k)
        compute(k)
        reduce_1(k)

    stages = steps[:-1] + [lambda k: (steps[-1](k), finish_sum(k))]
    stages += [gather_2, middle, reduce_2, reduce_3, reduce_4]
    stages += [functools.partial(spread, hop=hop) for hop in range(1, last + 1)]
    raw(0)
    for tick in range(len(stages) + last * (chunks - 1)):
        for k in reversed(range(chunks)):
            stage = tick - last * k
            if 0 <= stage < len(stages):
                stages[stage](k)
            if stage == len(stages) - last and k == chunks - 1:
                pick()

    for k in range(chunks):
        for d in range(replicas):
            pl.when((z > 0) & (z < d))(lambda: to_right(k, d).wait_send())
            pl.when((z < last) & (z > d))(lambda: to_left(k, d).wait_send())
            for p in range(2):
                pl.when((z < last) & (z >= d))(lambda: go_up(k, d, p).wait_send())
                pl.when((z > 0) & (z <= d))(lambda: go_down(k, d, p).wait_send())
            write(k, d).wait()
        share(k, 0, spot(me), sib).wait_send()
        share(k, 1, spot(me), near_x).wait_send()
        share(k, 2, spot(me), near_y).wait_send()
        share(k, 3, spot(near_x, 0, half), near_y).wait_send()
        share(k, 4, spot(near_y, half, half), near_x).wait_send()
        share(k, 5, spot(near_x), sib).wait_send()
        share(k, 6, spot(near_y), sib).wait_send()
        share(k, 7, spot(diag), sib).wait_send()
        for n in range(4):
            to_sib(k, n).wait_send()
            in_plane(k, n).wait_send()


def gram_kernel(size, block, left, right, new_left, new_right):
    g = block[0]
    scale = 0.1 / size
    f32 = dict(preferred_element_type=jnp.float32)
    left_gram = lax.dot_general(g, g, (((1,), (1,)), ((), ())), **f32)
    new_left[0] = 0.9 * left[0] + scale * left_gram
    right_gram = lax.dot_general(g, g, (((0,), (0,)), ((), ())), **f32)
    new_right[0] = 0.9 * right[0] + scale * right_gram


def line_body(grads, owner_map, factor_left, factor_right, left_roots, right_roots):
    replicas = lax.axis_size("replica")
    shards = lax.axis_size("shard")
    replica_at = lax.axis_index("replica")
    shard_at = lax.axis_index("shard")
    rows, columns = grads.shape[1:]
    capacity, size = factor_left.shape[1:3]
    block_rows, block_cols = owner_map.shape
    chunks = block_cols // replicas
    total_rows = rows * shards
    group = lax.dynamic_slice_in_dim(owner_map, replica_at * chunks, chunks, 1).T.reshape(-1)
    mine = group // capacity == shard_at
    slots = jnp.where(mine, group % capacity, 0)
    targets = shard_at * capacity + jnp.arange(capacity, dtype=jnp.int32)
    hits = group[None, :] == targets[:, None]
    place = jnp.sum(jnp.where(hits, jnp.arange(group.shape[0], dtype=jnp.int32), 0), axis=1)
    held = jnp.any(hits, axis=1).astype(jnp.int32)
    meta = jnp.concatenate([slots, mine.astype(jnp.int32), place, held])
    vmem = pl.BlockSpec(memory_space=pltpu.VMEM)
    smem = pl.BlockSpec(memory_space=pltpu.SMEM)
    hbm = pl.BlockSpec(memory_space=pl.ANY)
    dma = pltpu.SemaphoreType.DMA
    piece = (rows, size)
    bf16 = jnp.bfloat16
    update, picked = pl.pallas_call(
        functools.partial(exchange_kernel, replicas, chunks),
        out_shape=(
            jax.ShapeDtypeStruct((rows, columns), bf16),
            jax.ShapeDtypeStruct((capacity, size, size), bf16),
        ),
        in_specs=[smem] + [vmem] * 3,
        out_specs=(hbm, vmem),
        scratch_shapes=[pltpu.VMEM((chunks, replicas) + piece, WIRE)] * 4
        + [
            pltpu.VMEM((chunks * block_rows, size, size), bf16),
            pltpu.VMEM((chunks, total_rows, size), bf16),
        ]
        + [
            pltpu.VMEM((chunks, 4) + piece, bf16),
            pltpu.VMEM((chunks, 2, rows // 2, size), bf16),
            pltpu.VMEM((chunks, 2) + piece, bf16),
            pltpu.VMEM((block_cols,) + piece, bf16),
        ]
        + [dma((chunks, replicas))] * 4
        + [dma((chunks, 8))] * 2
        + [dma((chunks, 4))] * 4
        + [dma((block_cols, 2))] * 4
        + [dma((block_cols,))],
        compiler_params=pltpu.CompilerParams(
            collective_id=0, has_side_effects=True, vmem_limit_bytes=56 * 2**20
        ),
        name="exchange",
    )(meta, grads, left_roots, right_roots)

    square = pl.BlockSpec((1, size, size), lambda t: (t, 0, 0))
    factor = jax.ShapeDtypeStruct(factor_left.shape[1:], jnp.float32)
    new_left, new_right = pl.pallas_call(
        functools.partial(gram_kernel, size),
        out_shape=(factor, factor),
        grid=(capacity,),
        in_specs=[square] * 3,
        out_specs=(square, square),
        compiler_params=pltpu.CompilerParams(vmem_limit_bytes=32 * 2**20),
        name="grams",
    )(picked, factor_left[0], factor_right[0])
    return new_left[None], new_right[None], update


def solution(mesh):
    owned = P(("replica", "shard"), None, None, None)
    in_specs = (P("replica", "shard", None), P(), owned, owned, owned, owned)
    out_specs = (owned, owned, P("shard", None))
    body = line_body if dict(mesh.shape) == {"replica": 4, "shard": 8} else plain_body
    return jax.shard_map(body, mesh=mesh, in_specs=in_specs, out_specs=out_specs, check_vma=False)
```
